32 devices in a mesh: dp: 4 (over z), seq: 8 (over y, x, core).
Axes of the slice: x: 2, y: 2, z: 4, core: 2. Of those that a mesh axis runs over, the one named last changes fastest.
Arguments:
- queries: bfloat16 [32, 2, 128, 4096], P(('dp', 'seq')), parts along dimension 0, may hold values from -6 to 6
- key_heads: bfloat16 [32, 2, 128, 512], P(('dp', 'seq')), parts along dimension 0, may hold values from -6 to 6
- value_heads: bfloat16 [32, 2, 128, 512], P(('dp', 'seq')), parts along dimension 0, may hold values from -6 to 6
- out_grad: bfloat16 [32, 2, 128, 4096], P(('dp', 'seq')), parts along dimension 0, may hold values from -6 to 6
- doc_lengths: int32 [32], P('dp'), parts along dimension 0, may hold values from 1 to 384, 2048 in all
- block_reach: int32 [64], P('dp'), parts along dimension 0, may hold values from 0 to 3, as said below
Outputs:
- attended: bfloat16 [32, 2, 128, 4096], P(('dp', 'seq')), parts along dimension 0
- query_grad: bfloat16 [32, 2, 128, 4096], P(('dp', 'seq')), parts along dimension 0
- key_grad: bfloat16 [32, 2, 128, 512], P(('dp', 'seq')), parts along dimension 0
- value_grad: bfloat16 [32, 2, 128, 512], P(('dp', 'seq')), parts along dimension 0
The draws below stay inside these ranges and needn't reach their ends.
There are 4 independent parts, one for each index of `dp`. The reference program is written for one: setup_inputs(seed, part) draws one part's arguments, and reference() takes and returns one part's arrays. A program takes and returns all parts, laid end to end along the dimension named above; each array names one. Nothing has to cross between parts.
Inputs may be any that keep to these rules, and one draw needn't show every extreme that they name: doc_lengths are positive, sum to 2048, and the longest is exactly 384. `block_reach`: the value 4 - 1 occurs in every draw.
All inputs are finite; a program needn't handle non-finite values.
Results may differ from the reference program's by a relative error of at most 0.025.
Values may be sent and summed in bfloat16 or wider, within the bound.
A program may use at most 128 MiB of HBM per device.

```python
import math
import jax
import jax.numpy as jnp
import numpy as np
from jax import lax

BLOCK_TOKENS = 128
QUERY_HEADS = 32
KEY_VALUE_HEADS = 4
HEAD_SIZE = 128
WIN = 4
QW = 4096
KVW = 512
MIRROR_PAIRS = 8
BLOCKS = 16
SEQUENCE_TOKENS = 2048
DOCS = 8
MOSTLEN = 384


def sampled_pair_blocks(ordered):
    half_blocks = ordered.shape[0] // 2
    return jnp.stack([ordered[:half_blocks], ordered[half_blocks:][::-1]], axis=1)


def draw_queries(key, part):
    value_rows = jax.random.truncated_normal(jax.random.fold_in(key, 11), -6.0, 6.0, (SEQUENCE_TOKENS, QUERY_HEADS, HEAD_SIZE), jnp.float32)
    return sampled_pair_blocks(value_rows.reshape(2 * MIRROR_PAIRS, BLOCK_TOKENS, QUERY_HEADS * HEAD_SIZE)).astype(jnp.bfloat16)


def draw_key_heads(key, part):
    value_rows = jax.random.truncated_normal(jax.random.fold_in(key, 12), -6.0, 6.0, (SEQUENCE_TOKENS, KEY_VALUE_HEADS, HEAD_SIZE), jnp.float32)
    return sampled_pair_blocks(value_rows.reshape(2 * MIRROR_PAIRS, BLOCK_TOKENS, KEY_VALUE_HEADS * HEAD_SIZE)).astype(jnp.bfloat16)


def draw_block_reach(key, part):
    levels = jax.random.randint(jax.random.fold_in(key, 21), (BLOCKS,), 0, WIN)
    chosen_block = jax.random.randint(jax.random.fold_in(key, 22), (), 0, BLOCKS)
    return jnp.where(jnp.arange(BLOCKS) == chosen_block, WIN - 1, levels).astype(jnp.int32)


def shard_levels(rng, extent, cuts, smallest, high):
    loudness, own = 1.0, jax.random.fold_in(rng, 6)
    for dim, shards_of in cuts:
        draws = jnp.exp(jax.random.uniform(jax.random.fold_in(own, dim), (shards_of,), jnp.float32, smallest / len(cuts), high / len(cuts)))
        loudness = loudness * jnp.repeat(draws, extent[dim] // shards_of).reshape([-1 if axis == dim else 1 for axis in range(len(extent))])
    return loudness


def length_profile(count, total, reach, skew):
    portions = [(1 << 20) // math.isqrt(grade ** skew) + 1 for grade in range(2, count + 1)]
    spare, given = total - reach - (count - 1), [1] * (count - 1)
    while spare > 0:
        movable = [i for i in range(count - 1) if given[i] < reach]
        whole, left = sum([portions[i] for i in movable]), spare
        for i in movable:
            more = min(reach - given[i], max(1, left * portions[i] // whole), spare)
            given[i] = given[i] + more
            spare = spare - more
    return np.array([reach] + given)


def uneven(key, count, total, reach, skew):
    if count == 2:
        one = jax.random.randint(key, (), max(1, total - reach), min(reach, total - 1) + 1)
        return jnp.stack([one, total - one])
    sizes = jnp.asarray(length_profile(count, total, reach, skew), jnp.int32)
    couples = (count - 1) // 2
    source_of, taker = sizes[1:1 + 2 * couples:2], sizes[2:2 + 2 * couples:2]
    room = jnp.minimum(source_of - 1, reach - taker)
    shifted = jax.random.randint(jax.random.fold_in(key, 1), (couples,), 0, 1 << 20) % (room + 1)
    sizes = sizes.at[1:1 + 2 * couples:2].set(source_of - shifted).at[2:2 + 2 * couples:2].set(taker + shifted)
    return sizes[jax.random.permutation(jax.random.fold_in(key, 2), count)]


def bell_draw(stream_key, shape, deviation, reach, cuts=(), kind=jnp.bfloat16):
    gain = shard_levels(stream_key, shape, cuts, -0.22, 0.18) if cuts else 1.0
    entries = jax.random.normal(stream_key, shape, jnp.float32) * deviation * gain
    return jnp.minimum(jnp.maximum(entries, -reach), reach).astype(kind)


def setup_inputs(seed: int = 0, part: int = 0) -> dict:
    key_list = jax.random.split(jax.random.key(seed), 7)
    part_splits = jax.random.split(jax.random.fold_in(key_list[6], part), 7)
    return {
        "queries": draw_queries(jax.random.fold_in(jax.random.fold_in(key_list[6], part), 71), part),
        "key_heads": draw_key_heads(jax.random.fold_in(jax.random.fold_in(key_list[6], part), 71), part),
        "value_heads": bell_draw(part_splits[2], (MIRROR_PAIRS, 2, BLOCK_TOKENS, KVW), 1.0, 6.0, ((0, 8),)),
        "out_grad": bell_draw(part_splits[3], (MIRROR_PAIRS, 2, BLOCK_TOKENS, QW), 1.0, 6.0, ((0, 8),)),
        "doc_lengths": uneven(part_splits[4], DOCS, SEQUENCE_TOKENS, MOSTLEN, 2).astype(jnp.int32),
        "block_reach": draw_block_reach(jax.random.fold_in(jax.random.fold_in(key_list[6], part), 71), part),
    }


masked_fill = -1e30


def to_sequence(paired):
    return jnp.concatenate([paired[:, 0], paired[::-1, 1]], axis=0)


def to_pairs(ordered):
    half_blocks = ordered.shape[0] // 2
    return jnp.stack([ordered[:half_blocks], ordered[half_blocks:][::-1]], axis=1)


def doc_index(positions, doc_ends):
    return jnp.sum((positions[:, None] >= doc_ends[None, :]).astype(jnp.int32), axis=1)


def attend(queries_blk, grads_blk, key_window, value_window, first_key, block_index, reach_now, doc_ends):
    block_rows = queries_blk.shape[0]
    key_rows = key_window.shape[0]
    kv_width = key_window.shape[1]
    heads_kv = kv_width // HEAD_SIZE
    group_size = queries_blk.shape[1] // kv_width
    score_scale = HEAD_SIZE ** -0.5
    q_four = queries_blk.reshape(block_rows, heads_kv, group_size, HEAD_SIZE).astype(jnp.float32)
    g_four = grads_blk.reshape(block_rows, heads_kv, group_size, HEAD_SIZE).astype(jnp.float32)
    k_three = key_window.reshape(key_rows, heads_kv, HEAD_SIZE).astype(jnp.float32)
    v_three = value_window.reshape(key_rows, heads_kv, HEAD_SIZE).astype(jnp.float32)
    query_pos = block_index * block_rows + jnp.arange(block_rows, dtype=jnp.int32)
    key_pos = first_key + jnp.arange(key_rows, dtype=jnp.int32)
    allowed = (key_pos[None, :] <= query_pos[:, None]) & (key_pos[None, :] >= 0)
    allowed = allowed & (doc_index(key_pos, doc_ends)[None, :] == doc_index(query_pos, doc_ends)[:, None])
    allowed = allowed & (key_pos[None, :] // block_rows >= block_index - reach_now)
    scores = jnp.einsum("tkgd,skd->kgts", q_four, k_three) * score_scale
    masked = jnp.where(allowed, scores, masked_fill)
    row_max = jnp.max(masked, axis=-1, keepdims=True)
    row_sum = jnp.sum(jnp.exp(masked - row_max), axis=-1, keepdims=True)
    log_total = row_max + jnp.log(row_sum)
    weights = jnp.exp(masked - log_total)
    weights_low = weights.astype(jnp.bfloat16)
    attended = jnp.einsum("kgts,skd->tkgd", weights_low.astype(jnp.float32), v_three).astype(jnp.bfloat16)
    row_delta = jnp.einsum("tkgd,tkgd->kgt", g_four, attended.astype(jnp.float32))
    weight_grad = jnp.einsum("tkgd,skd->kgts", g_four, v_three)
    score_grad = (weights * (weight_grad - row_delta[..., None]) * score_scale).astype(jnp.bfloat16)
    query_grad = jnp.einsum("kgts,skd->tkgd", score_grad.astype(jnp.float32), k_three).astype(jnp.bfloat16)
    key_part = jnp.einsum("kgts,tkgd->skd", score_grad.astype(jnp.float32), q_four)
    value_part = jnp.einsum("kgts,tkgd->skd", weights_low.astype(jnp.float32), g_four)
    return (attended.reshape(block_rows, -1), query_grad.reshape(block_rows, -1),
            key_part.reshape(key_rows, kv_width), value_part.reshape(key_rows, kv_width))


def reference(queries, key_heads, value_heads, out_grad, doc_lengths, block_reach):
    doc_ends = jnp.cumsum(doc_lengths).astype(jnp.int32)
    query_seq = to_sequence(queries)
    grad_seq = to_sequence(out_grad)
    key_seq = to_sequence(key_heads)
    value_seq = to_sequence(value_heads)
    kv_width = key_seq.shape[-1]
    padding = jnp.zeros((WIN - 1, BLOCK_TOKENS, kv_width), key_seq.dtype)
    key_padded = jnp.concatenate([padding, key_seq], axis=0)
    value_padded = jnp.concatenate([padding, value_seq], axis=0)

    def one_block(block_index):
        key_window = lax.dynamic_slice_in_dim(key_padded, block_index, WIN, 0).reshape(WIN * BLOCK_TOKENS, kv_width)
        value_window = lax.dynamic_slice_in_dim(value_padded, block_index, WIN, 0).reshape(WIN * BLOCK_TOKENS, kv_width)
        reach_now = lax.dynamic_index_in_dim(block_reach, block_index, keepdims=False)
        queries_blk = lax.dynamic_index_in_dim(query_seq, block_index, keepdims=False)
        grads_blk = lax.dynamic_index_in_dim(grad_seq, block_index, keepdims=False)
        return attend(queries_blk, grads_blk, key_window, value_window,
                      (block_index - WIN + 1) * BLOCK_TOKENS, block_index, reach_now, doc_ends)

    block_ids = jnp.arange(2 * MIRROR_PAIRS, dtype=jnp.int32)
    attended, query_grad, key_parts, value_parts = lax.map(one_block, block_ids)
    key_parts = key_parts.reshape(2 * MIRROR_PAIRS, WIN, BLOCK_TOKENS, kv_width)
    value_parts = value_parts.reshape(2 * MIRROR_PAIRS, WIN, BLOCK_TOKENS, kv_width)
    key_total = jnp.zeros((2 * MIRROR_PAIRS + WIN - 1, BLOCK_TOKENS, kv_width), jnp.float32)
    value_total = jnp.zeros((2 * MIRROR_PAIRS + WIN - 1, BLOCK_TOKENS, kv_width), jnp.float32)
    for offset in range(WIN):
        key_total = key_total.at[offset:offset + 2 * MIRROR_PAIRS].add(key_parts[:, offset])
        value_total = value_total.at[offset:offset + 2 * MIRROR_PAIRS].add(value_parts[:, offset])
    key_grad = to_pairs(key_total[WIN - 1:].astype(jnp.bfloat16))
    value_grad = to_pairs(value_total[WIN - 1:].astype(jnp.bfloat16))
    return (to_pairs(attended), to_pairs(query_grad), key_grad, value_grad)
```

```python
import functools

import jax
import jax.numpy as jnp
from jax import lax
from jax.experimental import pallas as pl
from jax.experimental.pallas import tpu as pltpu
from jax.sharding import PartitionSpec as P

HEAD_SIZE = 128
WIN = 4
NEG = -1e30
LOG2E = 1.4426950408889634
MESH = pl.DeviceIdType.MESH


def kernel(n, heads_kv, group, rows, docs,
           len_ref, reach_ref, q_hbm, k_hbm, v_hbm, g_hbm,
           att_hbm, dq_hbm, dk_ref, dv_ref,
           win, q_s, g_s, att_s, dq_s, bias, p_s, ds_s, acc, pout, s1, fin,
           own_sem, in_sem, out_sem, kv_send, kv_recv, p_send, p_recv):
    d = lax.axis_index("seq")
    odd = lax.rem(d, 2) == 1
    even = jnp.logical_not(odd)
    sib = d + 1 - 2 * lax.rem(d, 2)
    width = group * HEAD_SIZE
    scale = HEAD_SIZE ** (-0.5)

    def cols(h, size):
        return pl.ds(pl.multiple_of(h * size, size), size)

    def own_copy(slot, which, h):
        src = (k_hbm, v_hbm)[which]
        return pltpu.make_async_copy(
            src.at[0, slot, :, cols(h, HEAD_SIZE)], win.at[4 * slot, h, which],
            own_sem.at[slot, which, h])

    def in_copy(which, slot, h):
        src, dst = ((q_hbm, q_s), (g_hbm, g_s))[which]
        return pltpu.make_async_copy(
            src.at[0, slot, :, cols(h, width)], dst.at[h, slot], in_sem.at[which, slot, h])

    def out_copy(which, slot, h):
        src, dst = ((att_s, att_hbm), (dq_s, dq_hbm))[which]
        return pltpu.make_async_copy(
            src.at[h, slot], dst.at[0, slot, :, cols(h, width)], out_sem.at[which, slot, h])

    def remote(src, dst, send_sem, recv_sem, target):
        return pltpu.make_async_remote_copy(
            src_ref=src, dst_ref=dst, send_sem=send_sem, recv_sem=recv_sem,
            device_id={"seq": target}, device_id_type=MESH)

    def kv(src, dst, kind, h, target):
        return remote(win.at[src, h], win.at[dst, h], kv_send.at[kind, h], kv_recv.at[dst, h],
                      target)

    kv_direct = (
        (d + 2 <= n - 1, 0, 2, 0, d + 2),
        (d >= 2, 4, 6, 1, d - 2),
        (jnp.logical_and(odd, d + 3 <= n - 1), 0, 3, 2, d + 3),
        (even, 0, 1, 2, sib),
        (jnp.logical_and(even, d >= 3), 4, 7, 3, d - 3),
        (odd, 4, 5, 3, sib),
        (d == n - 1, 0, 6, 6, d - 1),
        (d == n - 1, 0, 7, 7, d - 2),
    )
    kv_relay = (
        (jnp.logical_and(even, d >= 2), 2, 3, 4, sib),
        (jnp.logical_and(odd, d >= 2), 2, 1, 4, sib),
        (jnp.logical_and(odd, d + 2 <= n - 1), 6, 7, 5, sib),
        (jnp.logical_and(even, d + 2 <= n - 1), 6, 5, 5, sib),
    )

    def start_kv(table, h):
        for cond, src, dst, kind, target in table:
            @pl.when(cond)
            def _(src=src, dst=dst, kind=kind, target=target):
                kv(src, dst, kind, h, target).start()

    def wait_kv(cond, slot, h):
        @pl.when(cond)
        def _():
            kv(slot, slot, 0, h, sib).wait_recv()

    direct_in = (
        (d >= 2, 2), (d <= n - 2, 6), (odd, 1), (jnp.logical_and(even, d >= 3), 3),
        (even, 5),
        (jnp.logical_and(odd, d <= n - 3), 7),
    )
    relay_in = (
        (jnp.logical_and(even, d >= 2), 1), (jnp.logical_and(odd, d >= 3), 3),
        (jnp.logical_and(odd, d <= n - 2), 5),
        (jnp.logical_and(even, d <= n - 4), 7),
    )

    def part(src, kind, h, target):
        dst = s1.at[kind, h] if kind < 2 else fin.at[kind - 2, h]
        return remote(pout.at[src, h], dst, p_send.at[kind, h], p_recv.at[kind, h], target)

    part_first = (
        (jnp.logical_and(even, d >= 2), 1, 0, sib),
        (jnp.logical_and(odd, d >= 2), 3, 0, sib),
        (jnp.logical_and(odd, d <= n - 3), 5, 1, sib),
        (jnp.logical_and(even, d <= n - 3), 7, 1, sib),
        (jnp.logical_and(even, d >= 3), 3, 3, d - 3),
        (odd, 1, 3, sib),
        (jnp.logical_and(odd, d + 3 <= n - 1), 7, 5, d + 3),
        (even, 5, 5, sib),
        (d == n - 2, 6, 6, sib),
        (d == n - 3, 7, 7, d + 2),
    )
    part_second = (
        (d >= 2, 2, 2, d - 2),
        (d <= n - 3, 6, 4, d + 2),
    )
    fin_in = (
        (d <= n - 3, 2),
        (jnp.logical_or(even, d + 3 <= n - 1), 3),
        (d >= 2, 4),
        (jnp.logical_or(odd, d >= 3), 5),
        (d == n - 1, 6),
        (d == n - 1, 7),
    )

    def start_part(table, h):
        for cond, src, kind, target in table:
            @pl.when(cond)
            def _(src=src, kind=kind, target=target):
                part(src, kind, h, target).start()

    def wait_part(cond, kind, h):
        @pl.when(cond)
        def _():
            part(2, kind, h, sib).wait_recv()

    for h in range(heads_kv):
        for slot in range(2):
            for which in range(2):
                own_copy(slot, which, h).start()
    for h in range(heads_kv):
        for slot in range(2):
            for which in range(2):
                in_copy(which, slot, h).start()

    for slot in (1, 2, 3, 5, 6, 7):
        win[slot] = jnp.zeros(win.shape[1:], win.dtype)
    fin[...] = jnp.zeros(fin.shape, fin.dtype)

    barrier = pltpu.get_barrier_semaphore()
    partners = (
        (d >= 0, sib), (d >= 2, d - 2), (d + 2 <= n - 1, d + 2),
        (jnp.logical_and(odd, d + 3 <= n - 1), d + 3),
        (jnp.logical_and(even, d >= 3), d - 3),
    )
    for cond, target in partners:
        @pl.when(cond)
        def _(target=target):
            pl.semaphore_signal(barrier, inc=1, device_id={"seq": target}, device_id_type=MESH)
    peers = jnp.int32(0)
    for cond, _t in partners:
        peers = peers + jnp.where(cond, 1, 0)
    pl.semaphore_wait(barrier, peers)

    for h in range(heads_kv):
        for slot in range(2):
            for which in range(2):
                own_copy(slot, which, h).wait()
        start_kv(kv_direct, h)

    for slot, block in ((0, d), (1, 2 * n - 1 - d)):
        pos = block * rows + lax.broadcasted_iota(jnp.int32, (rows, 1), 0)
        first = jnp.zeros((rows, 1), jnp.int32)
        end = jnp.int32(0)
        for i in range(docs):
            end = end + len_ref[i]
            first = jnp.where(pos >= end, end, first)
        first = jnp.maximum(first, (block - reach_ref[block]) * rows)
        key = (block - WIN + 1) * rows + lax.broadcasted_iota(jnp.int32, (rows, WIN * rows), 1)
        ok = jnp.logical_and(key <= pos, key >= first)
        bias[slot] = jnp.where(ok, 0.0, NEG)

    last = d == n - 1
    slot_of = (
        (0, 1, 2, 3),
        (4, jnp.where(last, 0, 5), jnp.where(last, 1, 6),
         jnp.where(last, 2, jnp.where(d == n - 2, 0, 7))),
    )

    def stage_second(h):
        wait_part(d >= 2, 0, h)
        wait_part(d <= n - 3, 1, h)

        @pl.when(d >= 2)
        def _():
            pout[2, h] = (acc[h, 2] + s1[0, h].astype(jnp.float32)).astype(pout.dtype)

        @pl.when(d <= n - 3)
        def _():
            pout[6, h] = (acc[h, 6] + s1[1, h].astype(jnp.float32)).astype(pout.dtype)
        start_part(part_second, h)

    def compute(h, slot):
        index = slot_of[slot]
        k_win = jnp.concatenate([win[index[3 - j], h, 0] for j in range(WIN)], axis=0)
        v_win = jnp.concatenate([win[index[3 - j], h, 1] for j in range(WIN)], axis=0)
        nt = (((1,), (1,)), ((), ()))
        for i in range(group):
            at = slice(i * HEAD_SIZE, (i + 1) * HEAD_SIZE)
            rs = slice(i * rows, (i + 1) * rows)
            q = q_s[h, slot, :, at]
            g = g_s[h, slot, :, at]
            s = lax.dot_general(q, k_win, nt, preferred_element_type=jnp.float32) + bias[slot]
            top = jnp.max(s, axis=-1, keepdims=True)
            e = jnp.exp2((s - top) * (scale * LOG2E))
            w = e * (1.0 / jnp.sum(e, axis=-1, keepdims=True))
            low = w.astype(jnp.bfloat16)
            p_s[rs, :] = low
            att = jnp.dot(low, v_win, preferred_element_type=jnp.float32).astype(jnp.bfloat16)
            att_s[h, slot, :, at] = att
            delta = jnp.sum(g.astype(jnp.float32) * att.astype(jnp.float32), axis=-1,
                            keepdims=True)
            wg = lax.dot_general(g, v_win, nt, preferred_element_type=jnp.float32)
            ds = (w * (wg - delta)).astype(jnp.bfloat16)
            ds_s[rs, :] = ds
            dq = jnp.dot(ds, k_win, preferred_element_type=jnp.float32) * scale
            dq_s[h, slot, :, at] = dq.astype(jnp.bfloat16)
        q_all = jnp.concatenate(
            [q_s[h, slot, :, i * HEAD_SIZE:(i + 1) * HEAD_SIZE] for i in range(group)], axis=0)
        g_all = jnp.concatenate(
            [g_s[h, slot, :, i * HEAD_SIZE:(i + 1) * HEAD_SIZE] for i in range(group)], axis=0)
        tn = (((0,), (0,)), ((), ()))
        dk = lax.dot_general(ds_s[...], q_all, tn, preferred_element_type=jnp.float32) * scale
        dv = lax.dot_general(p_s[...], g_all, tn, preferred_element_type=jnp.float32)
        for j in range(WIN):
            at = slice((3 - j) * rows, (4 - j) * rows)
            acc[h, index[j], 0] += dk[at]
            acc[h, index[j], 1] += dv[at]

    for cond, slot in direct_in:
        wait_kv(cond, slot, 0)
    start_kv(kv_relay, 0)

    def step(h, carry):
        @pl.when(h + 1 < heads_kv)
        def _():
            for cond, slot in direct_in:
                wait_kv(cond, slot, h + 1)
            start_kv(kv_relay, h + 1)
        for cond, slot in relay_in:
            wait_kv(cond, slot, h)
        acc[h] = jnp.zeros(acc.shape[1:], acc.dtype)
        for slot in range(2):
            in_copy(0, slot, h).wait()
            in_copy(1, slot, h).wait()
            compute(h, slot)
            out_copy(0, slot, h).start()
            out_copy(1, slot, h).start()
        for slot in (1, 3, 5, 7):
            pout[slot, h] = acc[h, slot].astype(pout.dtype)

        @pl.when(d == n - 2)
        def _():
            pout[6, h] = acc[h, 6].astype(pout.dtype)
        start_part(part_first, h)

        @pl.when(h >= 1)
        def _():
            stage_second(h - 1)
        return carry

    lax.fori_loop(0, heads_kv, step, 0)
    stage_second(heads_kv - 1)

    for h in range(heads_kv):
        for cond, kind in fin_in:
            wait_part(cond, kind, h)
        f32 = jnp.float32
        low = acc[h, 0] + (fin[0, h].astype(f32) + fin[1, h].astype(f32)) + (
            fin[4, h].astype(f32) + fin[5, h].astype(f32))
        high = acc[h, 4] + (fin[2, h].astype(f32) + fin[3, h].astype(f32))
        at = slice(h * HEAD_SIZE, (h + 1) * HEAD_SIZE)
        for slot, total in ((0, low), (1, high)):
            dk_ref[0, slot, :, at] = total[0].astype(dk_ref.dtype)
            dv_ref[0, slot, :, at] = total[1].astype(dv_ref.dtype)

    for h in range(heads_kv):
        for slot in range(2):
            for which in range(2):
                out_copy(which, slot, h).wait()
        for cond, src, dst, kind, target in kv_direct + kv_relay:
            @pl.when(cond)
            def _(src=src, dst=dst, kind=kind, target=target):
                kv(src, dst, kind, h, target).wait_send()
        for cond, src, kind, target in part_first + part_second:
            @pl.when(cond)
            def _(src=src, kind=kind, target=target):
                part(src, kind, h, target).wait_send()


def shards(queries, key_heads, value_heads, out_grad, doc_lengths, block_reach):
    n = lax.axis_size("seq")
    rows = queries.shape[2]
    heads_kv = key_heads.shape[3] // HEAD_SIZE
    group = queries.shape[3] // key_heads.shape[3]
    width = group * HEAD_SIZE
    bf, f32 = jnp.bfloat16, jnp.float32
    tile = (2, rows, HEAD_SIZE)
    any_spec = pl.BlockSpec(memory_space=pl.ANY)
    smem = pl.BlockSpec(memory_space=pltpu.SMEM)
    vmem = pl.BlockSpec(memory_space=pltpu.VMEM)
    dma = pltpu.SemaphoreType.DMA
    flops = 2 * 6 * 2 * heads_kv * group * rows * WIN * rows * HEAD_SIZE
    return pl.pallas_call(
        functools.partial(kernel, n, heads_kv, group, rows, doc_lengths.shape[0]),
        out_shape=(
            jax.ShapeDtypeStruct(queries.shape, bf),
            jax.ShapeDtypeStruct(queries.shape, bf),
            jax.ShapeDtypeStruct(key_heads.shape, bf),
            jax.ShapeDtypeStruct(value_heads.shape, bf),
        ),
        in_specs=[smem, smem, any_spec, any_spec, any_spec, any_spec],
        out_specs=(any_spec, any_spec, vmem, vmem),
        scratch_shapes=[
            pltpu.VMEM((8, heads_kv) + tile, bf),
            pltpu.VMEM((heads_kv, 2, rows, width), bf),
            pltpu.VMEM((heads_kv, 2, rows, width), bf),
            pltpu.VMEM((heads_kv, 2, rows, width), bf),
            pltpu.VMEM((heads_kv, 2, rows, width), bf),
            pltpu.VMEM((2, rows, WIN * rows), f32),
            pltpu.VMEM((group * rows, WIN * rows), bf),
            pltpu.VMEM((group * rows, WIN * rows), bf),
            pltpu.VMEM((heads_kv, 8) + tile, f32),
            pltpu.VMEM((8, heads_kv) + tile, bf),
            pltpu.VMEM((2, heads_kv) + tile, bf),
            pltpu.VMEM((6, heads_kv) + tile, bf),
            dma((2, 2, heads_kv)),
            dma((2, 2, heads_kv)),
            dma((2, 2, heads_kv)),
            dma((8, heads_kv)),
            dma((8, heads_kv)),
            dma((8, heads_kv)),
            dma((8, heads_kv)),
        ],
        compiler_params=pltpu.CompilerParams(
            collective_id=0, has_side_effects=True, vmem_limit_bytes=52 * 1024 * 1024),
        cost_estimate=pl.CostEstimate(
            flops=flops, bytes_accessed=4 * queries.size * 2,
            transcendentals=2 * heads_kv * group * rows * WIN * rows),
    )(doc_lengths, block_reach, queries, key_heads, value_heads, out_grad)


def solution(mesh):
    split = P(("dp", "seq"), None, None, None)
    return jax.shard_map(
        shards, mesh=mesh, in_specs=(split, split, split, split, P("dp"), P("dp")),
        out_specs=(split, split, split, split), check_vma=False)
```

```python
import functools

import jax
import jax.numpy as jnp
from jax import lax
from jax.experimental import pallas as pl
from jax.experimental.pallas import tpu as pltpu
from jax.sharding import PartitionSpec as P

HEAD_SIZE = 128
WIN = 4
NEG = -1e30
LOG2E = 1.4426950408889634
MESH = pl.DeviceIdType.MESH


def kernel(n, heads_kv, group, rows, docs,
           len_ref, reach_ref, q_hbm, k_hbm, v_hbm, g_hbm,
           att_hbm, dq_hbm, dk_ref, dv_ref,
           win, q_s, g_s, att_s, dq_s, bias, sc_s, wg_s, p_s, ds_s, acc, pout, s1, fin,
           own_sem, in_sem, out_sem, kv_send, kv_recv, p_send, p_recv):
    d = lax.axis_index("seq")
    odd = lax.rem(d, 2) == 1
    even = jnp.logical_not(odd)
    sib = d + 1 - 2 * lax.rem(d, 2)
    width = group * HEAD_SIZE
    scale = HEAD_SIZE ** (-0.5)

    def cols(h, size):
        return pl.ds(pl.multiple_of(h * size, size), size)

    def own_copy(slot, which, h):
        src = (k_hbm, v_hbm)[which]
        return pltpu.make_async_copy(
            src.at[0, slot, :, cols(h, HEAD_SIZE)], win.at[4 * slot, h, which],
            own_sem.at[slot, which, h])

    def in_copy(which, slot, h):
        src, dst = ((q_hbm, q_s), (g_hbm, g_s))[which]
        return pltpu.make_async_copy(
            src.at[0, slot, :, cols(h, width)], dst.at[h, slot], in_sem.at[which, slot, h])

    def out_copy(which, slot, h):
        src, dst = ((att_s, att_hbm), (dq_s, dq_hbm))[which]
        return pltpu.make_async_copy(
            src.at[h, slot], dst.at[0, slot, :, cols(h, width)], out_sem.at[which, slot, h])

    def remote(src, dst, send_sem, recv_sem, target):
        return pltpu.make_async_remote_copy(
            src_ref=src, dst_ref=dst, send_sem=send_sem, recv_sem=recv_sem,
            device_id={"seq": target}, device_id_type=MESH)

    def kv(src, dst, kind, h, target):
        return remote(win.at[src, h], win.at[dst, h], kv_send.at[kind, h], kv_recv.at[dst, h],
                      target)

    kv_direct = (
        (d + 2 <= n - 1, 0, 2, 0, d + 2),
        (d >= 2, 4, 6, 1, d - 2),
        (jnp.logical_and(odd, d + 3 <= n - 1), 0, 3, 2, d + 3),
        (even, 0, 1, 2, sib),
        (jnp.logical_and(even, d >= 3), 4, 7, 3, d - 3),
        (odd, 4, 5, 3, sib),
        (d == n - 1, 0, 6, 6, d - 1),
        (d == n - 1, 0, 7, 7, d - 2),
    )
    kv_relay = (
        (jnp.logical_and(even, d >= 2), 2, 3, 4, sib),
        (jnp.logical_and(odd, d >= 2), 2, 1, 4, sib),
        (jnp.logical_and(odd, d + 2 <= n - 1), 6, 7, 5, sib),
        (jnp.logical_and(even, d + 2 <= n - 1), 6, 5, 5, sib),
    )

    def start_kv(table, h):
        for cond, src, dst, kind, target in table:
            @pl.when(cond)
            def _(src=src, dst=dst, kind=kind, target=target):
                kv(src, dst, kind, h, target).start()

    def wait_kv(cond, slot, h):
        @pl.when(cond)
        def _():
            kv(slot, slot, 0, h, sib).wait_recv()

    direct_in = (
        (d >= 2, 2), (d <= n - 2, 6), (odd, 1), (jnp.logical_and(even, d >= 3), 3),
        (even, 5),
        (jnp.logical_and(odd, d <= n - 3), 7),
    )
    relay_in = (
        (jnp.logical_and(even, d >= 2), 1), (jnp.logical_and(odd, d >= 3), 3),
        (jnp.logical_and(odd, d <= n - 2), 5),
        (jnp.logical_and(even, d <= n - 4), 7),
    )

    def part(src, kind, h, target):
        dst = s1.at[kind, h] if kind < 2 else fin.at[kind - 2, h]
        return remote(pout.at[src, h], dst, p_send.at[kind, h], p_recv.at[kind, h], target)

    part_first = (
        (jnp.logical_and(even, d >= 2), 1, 0, sib),
        (jnp.logical_and(odd, d >= 2), 3, 0, sib),
        (jnp.logical_and(odd, d <= n - 3), 5, 1, sib),
        (jnp.logical_and(even, d <= n - 3), 7, 1, sib),
        (jnp.logical_and(even, d >= 3), 3, 3, d - 3),
        (odd, 1, 3, sib),
        (jnp.logical_and(odd, d + 3 <= n - 1), 7, 5, d + 3),
        (even, 5, 5, sib),
        (d == n - 2, 6, 6, sib),
        (d == n - 3, 7, 7, d + 2),
    )
    part_second = (
        (d >= 2, 2, 2, d - 2),
        (d <= n - 3, 6, 4, d + 2),
    )
    fin_in = (
        (d <= n - 3, 2),
        (jnp.logical_or(even, d + 3 <= n - 1), 3),
        (d >= 2, 4),
        (jnp.logical_or(odd, d >= 3), 5),
        (d == n - 1, 6),
        (d == n - 1, 7),
    )

    def start_part(table, h):
        for cond, src, kind, target in table:
            @pl.when(cond)
            def _(src=src, kind=kind, target=target):
                part(src, kind, h, target).start()

    def wait_part(cond, kind, h):
        @pl.when(cond)
        def _():
            part(2, kind, h, sib).wait_recv()

    for h in range(heads_kv):
        for slot in range(2):
            for which in range(2):
                own_copy(slot, which, h).start()
    for h in range(heads_kv):
        for slot in range(2):
            for which in range(2):
                in_copy(which, slot, h).start()

    for slot in (1, 2, 3, 5, 6, 7):
        win[slot] = jnp.zeros(win.shape[1:], win.dtype)
    fin[...] = jnp.zeros(fin.shape, fin.dtype)

    barrier = pltpu.get_barrier_semaphore()
    partners = (
        (d >= 0, sib), (d >= 2, d - 2), (d + 2 <= n - 1, d + 2),
        (jnp.logical_and(odd, d + 3 <= n - 1), d + 3),
        (jnp.logical_and(even, d >= 3), d - 3),
    )
    for cond, target in partners:
        @pl.when(cond)
        def _(target=target):
            pl.semaphore_signal(barrier, inc=1, device_id={"seq": target}, device_id_type=MESH)
    peers = jnp.int32(0)
    for cond, _t in partners:
        peers = peers + jnp.where(cond, 1, 0)
    pl.semaphore_wait(barrier, peers)

    for h in range(heads_kv):
        for slot in range(2):
            for which in range(2):
                own_copy(slot, which, h).wait()
        start_kv(kv_direct, h)

    for slot, block in ((0, d), (1, 2 * n - 1 - d)):
        pos = block * rows + lax.broadcasted_iota(jnp.int32, (rows, 1), 0)
        first = jnp.zeros((rows, 1), jnp.int32)
        end = jnp.int32(0)
        for i in range(docs):
            end = end + len_ref[i]
            first = jnp.where(pos >= end, end, first)
        first = jnp.maximum(first, (block - reach_ref[block]) * rows)
        key = (block - WIN + 1) * rows + lax.broadcasted_iota(jnp.int32, (rows, WIN * rows), 1)
        ok = jnp.logical_and(key <= pos, key >= first)
        bias[slot] = jnp.where(ok, 0.0, NEG)

    last = d == n - 1
    slot_of = (
        (0, 1, 2, 3),
        (4, jnp.where(last, 0, 5), jnp.where(last, 1, 6),
         jnp.where(last, 2, jnp.where(d == n - 2, 0, 7))),
    )

    def stage_second(h):
        wait_part(d >= 2, 0, h)
        wait_part(d <= n - 3, 1, h)

        @pl.when(d >= 2)
        def _():
            pout[2, h] = (acc[h, 2] + s1[0, h].astype(jnp.float32)).astype(pout.dtype)

        @pl.when(d <= n - 3)
        def _():
            pout[6, h] = (acc[h, 6] + s1[1, h].astype(jnp.float32)).astype(pout.dtype)
        start_part(part_second, h)

    nt = (((1,), (1,)), ((), ()))
    tn = (((0,), (0,)), ((), ()))
    f32 = jnp.float32
    bf16 = jnp.bfloat16
    pair = 2 if group % 2 == 0 else 1
    units = group // pair
    urows = pair * rows
    trows = rows // 2

    def window(h, slot, which):
        index = slot_of[slot]
        return jnp.concatenate([win[index[3 - j], h, which] for j in range(WIN)], axis=0)

    def stacked(ref, h, slot, first, count):
        return jnp.concatenate(
            [ref[h, slot, :, i * HEAD_SIZE:(i + 1) * HEAD_SIZE]
             for i in range(first, first + count)], axis=0)

    def products(h, slot, u):
        rs = slice(u * urows, (u + 1) * urows)
        sc_s[slot, rs, :] = lax.dot_general(
            stacked(q_s, h, slot, u * pair, pair), window(h, slot, 0), nt,
            preferred_element_type=f32)
        wg_s[slot, rs, :] = lax.dot_general(
            stacked(g_s, h, slot, u * pair, pair), window(h, slot, 1), nt,
            preferred_element_type=f32)

    def weigh(slot, u):
        for t in range(urows // trows):
            rs = slice(u * urows + t * trows, u * urows + (t + 1) * trows)
            bs = slice((t * trows) % rows, (t * trows) % rows + trows)
            s = sc_s[slot, rs, :] + bias[slot, bs, :]
            top = jnp.max(s, axis=-1, keepdims=True)
            e = jnp.exp2((s - top) * (scale * LOG2E))
            wg = wg_s[slot, rs, :]
            inv = 1.0 / jnp.sum(e, axis=-1, keepdims=True)
            delta = jnp.sum(e * wg, axis=-1, keepdims=True) * inv
            w = e * inv
            p_s[slot, rs, :] = w.astype(bf16)
            ds_s[slot, rs, :] = (w * (wg - delta)).astype(bf16)

    def outputs(h, slot, u):
        rs = slice(u * urows, (u + 1) * urows)
        att = jnp.dot(p_s[slot, rs, :], window(h, slot, 1), preferred_element_type=f32)
        dq = jnp.dot(ds_s[slot, rs, :], window(h, slot, 0), preferred_element_type=f32) * scale
        for i in range(pair):
            at = slice((u * pair + i) * HEAD_SIZE, (u * pair + i + 1) * HEAD_SIZE)
            att_s[h, slot, :, at] = att[i * rows:(i + 1) * rows].astype(bf16)
            dq_s[h, slot, :, at] = dq[i * rows:(i + 1) * rows].astype(bf16)

    def partials(h, slot):
        index = slot_of[slot]
        dk = lax.dot_general(ds_s[slot], stacked(q_s, h, slot, 0, group), tn,
                             preferred_element_type=f32) * scale
        dv = lax.dot_general(p_s[slot], stacked(g_s, h, slot, 0, group), tn,
                             preferred_element_type=f32)
        for j in range(WIN):
            at = slice((3 - j) * rows, (4 - j) * rows)
            acc[h, index[j], 0] += dk[at]
            acc[h, index[j], 1] += dv[at]

    def compute(h):
        work = [(slot, u) for slot in range(2) for u in range(units)]
        products(h, *work[0])
        for i, (slot, u) in enumerate(work):
            if i + 1 < len(work):
                products(h, *work[i + 1])
            weigh(slot, u)
            if i:
                outputs(h, *work[i - 1])
                if work[i - 1][1] == units - 1:
                    partials(h, 0)
        outputs(h, *work[-1])
        partials(h, 1)

    for cond, slot in direct_in:
        wait_kv(cond, slot, 0)
    start_kv(kv_relay, 0)

    def step(h, carry):
        @pl.when(h + 1 < heads_kv)
        def _():
            for cond, slot in direct_in:
                wait_kv(cond, slot, h + 1)
            start_kv(kv_relay, h + 1)
        for cond, slot in relay_in:
            wait_kv(cond, slot, h)
        acc[h] = jnp.zeros(acc.shape[1:], acc.dtype)
        for slot in range(2):
            in_copy(0, slot, h).wait()
            in_copy(1, slot, h).wait()
        compute(h)
        for slot in range(2):
            out_copy(0, slot, h).start()
            out_copy(1, slot, h).start()
        for slot in (1, 3, 5, 7):
            pout[slot, h] = acc[h, slot].astype(pout.dtype)

        @pl.when(d == n - 2)
        def _():
            pout[6, h] = acc[h, 6].astype(pout.dtype)
        start_part(part_first, h)

        @pl.when(h >= 1)
        def _():
            stage_second(h - 1)
        return carry

    lax.fori_loop(0, heads_kv, step, 0)
    stage_second(heads_kv - 1)

    for h in range(heads_kv):
        for cond, kind in fin_in:
            wait_part(cond, kind, h)
        low = acc[h, 0] + (fin[0, h].astype(f32) + fin[1, h].astype(f32)) + (
            fin[4, h].astype(f32) + fin[5, h].astype(f32))
        high = acc[h, 4] + (fin[2, h].astype(f32) + fin[3, h].astype(f32))
        at = slice(h * HEAD_SIZE, (h + 1) * HEAD_SIZE)
        for slot, total in ((0, low), (1, high)):
            dk_ref[0, slot, :, at] = total[0].astype(dk_ref.dtype)
            dv_ref[0, slot, :, at] = total[1].astype(dv_ref.dtype)

    for h in range(heads_kv):
        for slot in range(2):
            for which in range(2):
                out_copy(which, slot, h).wait()
        for cond, src, dst, kind, target in kv_direct + kv_relay:
            @pl.when(cond)
            def _(src=src, dst=dst, kind=kind, target=target):
                kv(src, dst, kind, h, target).wait_send()
        for cond, src, kind, target in part_first + part_second:
            @pl.when(cond)
            def _(src=src, kind=kind, target=target):
                part(src, kind, h, target).wait_send()


def shards(queries, key_heads, value_heads, out_grad, doc_lengths, block_reach):
    n = lax.axis_size("seq")
    rows = queries.shape[2]
    heads_kv = key_heads.shape[3] // HEAD_SIZE
    group = queries.shape[3] // key_heads.shape[3]
    width = group * HEAD_SIZE
    bf, f32 = jnp.bfloat16, jnp.float32
    tile = (2, rows, HEAD_SIZE)
    any_spec = pl.BlockSpec(memory_space=pltpu.HBM)
    smem = pl.BlockSpec(memory_space=pltpu.SMEM)
    vmem = pl.BlockSpec(memory_space=pltpu.VMEM)
    dma = pltpu.SemaphoreType.DMA
    flops = 2 * 6 * 2 * heads_kv * group * rows * WIN * rows * HEAD_SIZE
    return pl.pallas_call(
        functools.partial(kernel, n, heads_kv, group, rows, doc_lengths.shape[0]),
        out_shape=(
            jax.ShapeDtypeStruct(queries.shape, bf),
            jax.ShapeDtypeStruct(queries.shape, bf),
            jax.ShapeDtypeStruct(key_heads.shape, bf),
            jax.ShapeDtypeStruct(value_heads.shape, bf),
        ),
        in_specs=[smem, smem, any_spec, any_spec, any_spec, any_spec],
        out_specs=(any_spec, any_spec, vmem, vmem),
        scratch_shapes=[
            pltpu.VMEM((8, heads_kv) + tile, bf),
            pltpu.VMEM((heads_kv, 2, rows, width), bf),
            pltpu.VMEM((heads_kv, 2, rows, width), bf),
            pltpu.VMEM((heads_kv, 2, rows, width), bf),
            pltpu.VMEM((heads_kv, 2, rows, width), bf),
            pltpu.VMEM((2, rows, WIN * rows), f32),
            pltpu.VMEM((2, group * rows, WIN * rows), f32),
            pltpu.VMEM((2, group * rows, WIN * rows), f32),
            pltpu.VMEM((2, group * rows, WIN * rows), bf),
            pltpu.VMEM((2, group * rows, WIN * rows), bf),
            pltpu.VMEM((heads_kv, 8) + tile, f32),
            pltpu.VMEM((8, heads_kv) + tile, bf),
            pltpu.VMEM((2, heads_kv) + tile, bf),
            pltpu.VMEM((6, heads_kv) + tile, bf),
            dma((2, 2, heads_kv)),
            dma((2, 2, heads_kv)),
            dma((2, 2, heads_kv)),
            dma((8, heads_kv)),
            dma((8, heads_kv)),
            dma((8, heads_kv)),
            dma((8, heads_kv)),
        ],
        compiler_params=pltpu.CompilerParams(
            collective_id=0, has_side_effects=True, vmem_limit_bytes=52 * 1024 * 1024),
        cost_estimate=pl.CostEstimate(
            flops=flops, bytes_accessed=4 * queries.size * 2,
            transcendentals=2 * heads_kv * group * rows * WIN * rows),
    )(doc_lengths, block_reach, queries, key_heads, value_heads, out_grad)


def solution(mesh):
    split = P(("dp", "seq"), None, None, None)
    return jax.shard_map(
        shards, mesh=mesh, in_specs=(split, split, split, split, P("dp"), P("dp")),
        out_specs=(split, split, split, split), check_vma=False)
```

```python
import functools

import jax
import jax.numpy as jnp
from jax import lax
from jax.experimental import pallas as pl
from jax.experimental.pallas import tpu as pltpu
from jax.sharding import PartitionSpec as P

HEAD_SIZE = 128
WIN = 4
NEG = -1e30
LOG2E = 1.4426950408889634
MESH = pl.DeviceIdType.MESH


def kernel(n, heads_kv, group, rows, docs,
           len_ref, reach_ref, q_hbm, k_hbm, v_hbm, g_hbm,
           att_hbm, dq_hbm, dk_ref, dv_ref,
           win, q_s, g_s, att_s, dq_s, bias, sc_s, wg_s, p_s, ds_s, acc, pout, s1, fin,
           own_sem, in_sem, out_sem, kv_send, kv_recv, p_send, p_recv):
    d = lax.axis_index("seq")
    odd = lax.rem(d, 2) == 1
    even = jnp.logical_not(odd)
    sib = d + 1 - 2 * lax.rem(d, 2)
    width = group * HEAD_SIZE
    scale = HEAD_SIZE ** (-0.5)

    def cols(h, size):
        return pl.ds(pl.multiple_of(h * size, size), size)

    def own_copy(slot, which, h):
        src = (k_hbm, v_hbm)[which]
        return pltpu.make_async_copy(
            src.at[0, slot, :, cols(h, HEAD_SIZE)], win.at[4 * slot, h, which],
            own_sem.at[slot, which, h])

    def in_copy(which, slot, h):
        src, dst = ((q_hbm, q_s), (g_hbm, g_s))[which]
        return pltpu.make_async_copy(
            src.at[0, slot, :, cols(h, width)], dst.at[h, slot], in_sem.at[which, slot, h])

    def out_copy(which, slot, h):
        src, dst = ((att_s, att_hbm), (dq_s, dq_hbm))[which]
        return pltpu.make_async_copy(
            src.at[h, slot], dst.at[0, slot, :, cols(h, width)], out_sem.at[which, slot, h])

    def remote(src, dst, send_sem, recv_sem, target):
        return pltpu.make_async_remote_copy(
            src_ref=src, dst_ref=dst, send_sem=send_sem, recv_sem=recv_sem,
            device_id={"seq": target}, device_id_type=MESH)

    def kv(src, dst, kind, h, target):
        return remote(win.at[src, h], win.at[dst, h], kv_send.at[kind, h], kv_recv.at[dst, h],
                      target)

    kv_direct = (
        (d + 2 <= n - 1, 0, 2, 0, d + 2),
        (d >= 2, 4, 6, 1, d - 2),
        (jnp.logical_and(odd, d + 3 <= n - 1), 0, 3, 2, d + 3),
        (even, 0, 1, 2, sib),
        (jnp.logical_and(even, d >= 3), 4, 7, 3, d - 3),
        (odd, 4, 5, 3, sib),
        (d == n - 1, 0, 6, 6, d - 1),
        (d == n - 1, 0, 7, 7, d - 2),
    )
    kv_relay = (
        (jnp.logical_and(even, d >= 2), 2, 3, 4, sib),
        (jnp.logical_and(odd, d >= 2), 2, 1, 4, sib),
        (jnp.logical_and(odd, d + 2 <= n - 1), 6, 7, 5, sib),
        (jnp.logical_and(even, d + 2 <= n - 1), 6, 5, 5, sib),
    )

    def start_kv(table, h):
        for cond, src, dst, kind, target in table:
            @pl.when(cond)
            def _(src=src, dst=dst, kind=kind, target=target):
                kv(src, dst, kind, h, target).start()

    def wait_kv(cond, slot, h):
        @pl.when(cond)
        def _():
            kv(slot, slot, 0, h, sib).wait_recv()

    direct_in = (
        (d >= 2, 2), (d <= n - 2, 6), (odd, 1), (jnp.logical_and(even, d >= 3), 3),
        (even, 5),
        (jnp.logical_and(odd, d <= n - 3), 7),
    )
    relay_in = (
        (jnp.logical_and(even, d >= 2), 1), (jnp.logical_and(odd, d >= 3), 3),
        (jnp.logical_and(odd, d <= n - 2), 5),
        (jnp.logical_and(even, d <= n - 4), 7),
    )

    def part(src, kind, h, target):
        dst = s1.at[kind, h] if kind < 2 else fin.at[kind - 2, h]
        return remote(pout.at[src, h], dst, p_send.at[kind, h], p_recv.at[kind, h], target)

    part_low = (
        (jnp.logical_and(even, d >= 2), 1, 0, sib),
        (jnp.logical_and(odd, d >= 2), 3, 0, sib),
        (jnp.logical_and(even, d >= 3), 3, 3, d - 3),
        (odd, 1, 3, sib),
    )
    part_high = (
        (jnp.logical_and(odd, d <= n - 3), 5, 1, sib),
        (jnp.logical_and(even, d <= n - 3), 7, 1, sib),
        (jnp.logical_and(odd, d + 3 <= n - 1), 7, 5, d + 3),
        (even, 5, 5, sib),
        (d == n - 2, 6, 6, sib),
        (d == n - 3, 7, 7, d + 2),
    )
    part_second = (
        (d >= 2, 2, 2, d - 2),
        (d <= n - 3, 6, 4, d + 2),
    )
    fin_in = (
        (d <= n - 3, 2),
        (jnp.logical_or(even, d + 3 <= n - 1), 3),
        (d >= 2, 4),
        (jnp.logical_or(odd, d >= 3), 5),
        (d == n - 1, 6),
        (d == n - 1, 7),
    )

    def start_part(table, h):
        for cond, src, kind, target in table:
            @pl.when(cond)
            def _(src=src, kind=kind, target=target):
                part(src, kind, h, target).start()

    def wait_part(cond, kind, h):
        @pl.when(cond)
        def _():
            part(2, kind, h, sib).wait_recv()

    for h in range(heads_kv):
        for slot in range(2):
            for which in range(2):
                own_copy(slot, which, h).start()
    for h in range(heads_kv):
        for slot in range(2):
            for which in range(2):
                in_copy(which, slot, h).start()

    for slot in (1, 2, 3, 5, 6, 7):
        win[slot] = jnp.zeros(win.shape[1:], win.dtype)
    fin[...] = jnp.zeros(fin.shape, fin.dtype)

    barrier = pltpu.get_barrier_semaphore()
    partners = (
        (d >= 0, sib), (d >= 2, d - 2), (d + 2 <= n - 1, d + 2),
        (jnp.logical_and(odd, d + 3 <= n - 1), d + 3),
        (jnp.logical_and(even, d >= 3), d - 3),
    )
    for cond, target in partners:
        @pl.when(cond)
        def _(target=target):
            pl.semaphore_signal(barrier, inc=1, device_id={"seq": target}, device_id_type=MESH)
    peers = jnp.int32(0)
    for cond, _t in partners:
        peers = peers + jnp.where(cond, 1, 0)
    pl.semaphore_wait(barrier, peers)

    def send_own(h):
        for slot in range(2):
            for which in range(2):
                own_copy(slot, which, h).wait()
        start_kv(kv_direct, h)

    send_own(0)

    for slot, block in ((0, d), (1, 2 * n - 1 - d)):
        pos = block * rows + lax.broadcasted_iota(jnp.int32, (rows, 1), 0)
        first = jnp.zeros((rows, 1), jnp.int32)
        end = jnp.int32(0)
        for i in range(docs):
            end = end + len_ref[i]
            first = jnp.where(pos >= end, end, first)
        first = jnp.maximum(first, (block - reach_ref[block]) * rows)
        key = (block - WIN + 1) * rows + lax.broadcasted_iota(jnp.int32, (rows, WIN * rows), 1)
        ok = jnp.logical_and(key <= pos, key >= first)
        bias[slot] = jnp.where(ok, 0.0, NEG)

    last = d == n - 1
    slot_of = (
        (0, 1, 2, 3),
        (4, jnp.where(last, 0, 5), jnp.where(last, 1, 6),
         jnp.where(last, 2, jnp.where(d == n - 2, 0, 7))),
    )

    def stage_second(h):
        wait_part(d >= 2, 0, h)
        wait_part(d <= n - 3, 1, h)

        @pl.when(d >= 2)
        def _():
            pout[2, h] = (acc[h, 2] + s1[0, h].astype(jnp.float32)).astype(pout.dtype)

        @pl.when(d <= n - 3)
        def _():
            pout[6, h] = (acc[h, 6] + s1[1, h].astype(jnp.float32)).astype(pout.dtype)
        start_part(part_second, h)

    nt = (((1,), (1,)), ((), ()))
    tn = (((0,), (0,)), ((), ()))
    f32 = jnp.float32
    bf16 = jnp.bfloat16
    pair = 2 if group % 2 == 0 else 1
    units = group // pair
    urows = pair * rows
    trows = rows // 2

    def window(h, slot, which):
        index = slot_of[slot]
        return jnp.concatenate([win[index[3 - j], h, which] for j in range(WIN)], axis=0)

    def stacked(ref, h, slot, first, count):
        return jnp.concatenate(
            [ref[h, slot, :, i * HEAD_SIZE:(i + 1) * HEAD_SIZE]
             for i in range(first, first + count)], axis=0)

    def products(h, slot, u):
        rs = slice(u * urows, (u + 1) * urows)
        sc_s[slot, rs, :] = lax.dot_general(
            stacked(q_s, h, slot, u * pair, pair), window(h, slot, 0), nt,
            preferred_element_type=f32)
        wg_s[slot, rs, :] = lax.dot_general(
            stacked(g_s, h, slot, u * pair, pair), window(h, slot, 1), nt,
            preferred_element_type=f32)

    def weigh(slot, u):
        for t in range(urows // trows):
            rs = slice(u * urows + t * trows, u * urows + (t + 1) * trows)
            bs = slice((t * trows) % rows, (t * trows) % rows + trows)
            s = sc_s[slot, rs, :] + bias[slot, bs, :]
            top = jnp.max(s, axis=-1, keepdims=True)
            e = jnp.exp2((s - top) * (scale * LOG2E))
            wg = wg_s[slot, rs, :]
            inv = 1.0 / jnp.sum(e, axis=-1, keepdims=True)
            delta = jnp.sum(e * wg, axis=-1, keepdims=True) * inv
            w = e * inv
            p_s[slot, rs, :] = w.astype(bf16)
            ds_s[slot, rs, :] = (w * (wg - delta)).astype(bf16)

    def outputs(h, slot, u):
        rs = slice(u * urows, (u + 1) * urows)
        att = jnp.dot(p_s[slot, rs, :], window(h, slot, 1), preferred_element_type=f32)
        dq = jnp.dot(ds_s[slot, rs, :], window(h, slot, 0), preferred_element_type=f32) * scale
        for i in range(pair):
            at = slice((u * pair + i) * HEAD_SIZE, (u * pair + i + 1) * HEAD_SIZE)
            att_s[h, slot, :, at] = att[i * rows:(i + 1) * rows].astype(bf16)
            dq_s[h, slot, :, at] = dq[i * rows:(i + 1) * rows].astype(bf16)

    def partials(h, slot):
        index = slot_of[slot]
        dk = lax.dot_general(stacked(q_s, h, slot, 0, group), ds_s[slot], tn,
                             preferred_element_type=f32) * scale
        dv = lax.dot_general(stacked(g_s, h, slot, 0, group), p_s[slot], tn,
                             preferred_element_type=f32)
        for j in range(WIN):
            at = slice((3 - j) * rows, (4 - j) * rows)
            acc[h, index[j], 0] += dk[:, at].T
            acc[h, index[j], 1] += dv[:, at].T

    def half(h, slot, last_head):
        for u in range(units):
            if u + 1 < units:
                products(h, slot, u + 1)
            elif slot == 1:
                products(h, 0, 0)
            weigh(slot, u)
            if u and not last_head:
                outputs(h, slot, u - 1)
        partials(h, slot)
        if not last_head:
            outputs(h, slot, units - 1)

    def send_out(h, slot):
        out_copy(0, slot, h).start()
        out_copy(1, slot, h).start()

    def finish(h, slot):
        for u in range(units):
            outputs(h, slot, u)
        send_out(h, slot)

    def cast_parts(h, slots):
        for slot in slots:
            pout[slot, h] = acc[h, slot].astype(pout.dtype)

    for cond, slot in direct_in:
        wait_kv(cond, slot, 0)
    start_kv(kv_relay, 0)
    send_own(1)

    def step(h, last_head):
        for cond, slot in relay_in:
            wait_kv(cond, slot, h)
        if not last_head:
            @pl.when(h + 2 < heads_kv)
            def _():
                send_own(h + 2)
        acc[h] = jnp.zeros(acc.shape[1:], acc.dtype)
        for slot in range(2):
            in_copy(0, slot, h).wait()
            in_copy(1, slot, h).wait()
        products(h, 1, 0)
        half(h, 1, last_head)
        cast_parts(h, (5, 7))

        @pl.when(d == n - 2)
        def _():
            pout[6, h] = acc[h, 6].astype(pout.dtype)
        start_part(part_high, h)
        if last_head:
            stage_second(h - 1)
        else:
            send_out(h, 1)
            for cond, slot in direct_in:
                wait_kv(cond, slot, h + 1)
            start_kv(kv_relay, h + 1)

            @pl.when(h >= 1)
            def _():
                stage_second(h - 1)
        half(h, 0, last_head)
        cast_parts(h, (1, 3))
        start_part(part_low, h)
        if not last_head:
            send_out(h, 0)

    def body(h, carry):
        step(h, False)
        return carry

    end_head = heads_kv - 1
    lax.fori_loop(0, end_head, body, 0)
    step(end_head, True)
    finish(end_head, 1)
    stage_second(end_head)
    finish(end_head, 0)

    for h in range(heads_kv):
        for cond, kind in fin_in:
            wait_part(cond, kind, h)
        low = acc[h, 0] + (fin[0, h].astype(f32) + fin[1, h].astype(f32)) + (
            fin[4, h].astype(f32) + fin[5, h].astype(f32))
        high = acc[h, 4] + (fin[2, h].astype(f32) + fin[3, h].astype(f32))
        at = slice(h * HEAD_SIZE, (h + 1) * HEAD_SIZE)
        for slot, total in ((0, low), (1, high)):
            dk_ref[0, slot, :, at] = total[0].astype(dk_ref.dtype)
            dv_ref[0, slot, :, at] = total[1].astype(dv_ref.dtype)

    for h in range(heads_kv):
        for slot in range(2):
            for which in range(2):
                out_copy(which, slot, h).wait()
        for cond, src, dst, kind, target in kv_direct + kv_relay:
            @pl.when(cond)
            def _(src=src, dst=dst, kind=kind, target=target):
                kv(src, dst, kind, h, target).wait_send()
        for cond, src, kind, target in part_low + part_high + part_second:
            @pl.when(cond)
            def _(src=src, kind=kind, target=target):
                part(src, kind, h, target).wait_send()


def shards(queries, key_heads, value_heads, out_grad, doc_lengths, block_reach):
    n = lax.axis_size("seq")
    rows = queries.shape[2]
    heads_kv = key_heads.shape[3] // HEAD_SIZE
    group = queries.shape[3] // key_heads.shape[3]
    width = group * HEAD_SIZE
    bf, f32 = jnp.bfloat16, jnp.float32
    tile = (2, rows, HEAD_SIZE)
    any_spec = pl.BlockSpec(memory_space=pltpu.HBM)
    smem = pl.BlockSpec(memory_space=pltpu.SMEM)
    vmem = pl.BlockSpec(memory_space=pltpu.VMEM)
    dma = pltpu.SemaphoreType.DMA
    flops = 2 * 6 * 2 * heads_kv * group * rows * WIN * rows * HEAD_SIZE
    return pl.pallas_call(
        functools.partial(kernel, n, heads_kv, group, rows, doc_lengths.shape[0]),
        out_shape=(
            jax.ShapeDtypeStruct(queries.shape, bf),
            jax.ShapeDtypeStruct(queries.shape, bf),
            jax.ShapeDtypeStruct(key_heads.shape, bf),
            jax.ShapeDtypeStruct(value_heads.shape, bf),
        ),
        in_specs=[smem, smem, any_spec, any_spec, any_spec, any_spec],
        out_specs=(any_spec, any_spec, vmem, vmem),
        scratch_shapes=[
            pltpu.VMEM((8, heads_kv) + tile, bf),
            pltpu.VMEM((heads_kv, 2, rows, width), bf),
            pltpu.VMEM((heads_kv, 2, rows, width), bf),
            pltpu.VMEM((heads_kv, 2, rows, width), bf),
            pltpu.VMEM((heads_kv, 2, rows, width), bf),
            pltpu.VMEM((2, rows, WIN * rows), f32),
            pltpu.VMEM((2, group * rows, WIN * rows), f32),
            pltpu.VMEM((2, group * rows, WIN * rows), f32),
            pltpu.VMEM((2, group * rows, WIN * rows), bf),
            pltpu.VMEM((2, group * rows, WIN * rows), bf),
            pltpu.VMEM((heads_kv, 8) + tile, f32),
            pltpu.VMEM((8, heads_kv) + tile, bf),
            pltpu.VMEM((2, heads_kv) + tile, bf),
            pltpu.VMEM((6, heads_kv) + tile, bf),
            dma((2, 2, heads_kv)),
            dma((2, 2, heads_kv)),
            dma((2, 2, heads_kv)),
            dma((8, heads_kv)),
            dma((8, heads_kv)),
            dma((8, heads_kv)),
            dma((8, heads_kv)),
        ],
        compiler_params=pltpu.CompilerParams(
            collective_id=0, has_side_effects=True, vmem_limit_bytes=63 * 1024 * 1024),
        cost_estimate=pl.CostEstimate(
            flops=flops, bytes_accessed=4 * queries.size * 2,
            transcendentals=2 * heads_kv * group * rows * WIN * rows),
    )(doc_lengths, block_reach, queries, key_heads, value_heads, out_grad)


def solution(mesh):
    split = P(("dp", "seq"), None, None, None)
    return jax.shard_map(
        shards, mesh=mesh, in_specs=(split, split, split, split, P("dp"), P("dp")),
        out_specs=(split, split, split, split), check_vma=False)
```
